128 devices in a mesh: seq: 16 (over x, y), grp: 8 (over z, core).
Axes of the slice: x: 4, y: 4, z: 4, core: 2. Of those that a mesh axis runs over, the one named last changes fastest.
Arguments:
- video: bfloat16 [65536, 1536], P(('grp', 'seq')), parts along dimension 0, may hold values from -28 to 28
- audio: bfloat16 [8192, 1536], P(('grp', 'seq')), parts along dimension 0, may hold values from -28 to 28
- wq_video: bfloat16 [1536, 1536], replicated, may hold values from -0.3125 to 0.3125
- wk_video: bfloat16 [1536, 1536], replicated, may hold values from -0.15625 to 0.15625
- wv_video: bfloat16 [1536, 1536], replicated, may hold values from -0.15625 to 0.15625
- wo_video: bfloat16 [1536, 1536], replicated, may hold values from -0.875 to 0.875
- wq_audio: bfloat16 [1536, 1536], P('seq'), may hold values from -0.3125 to 0.3125
- wk_audio: bfloat16 [1536, 1536], P('seq'), may hold values from -0.15625 to 0.15625
- wv_audio: bfloat16 [1536, 1536], P('seq'), may hold values from -0.15625 to 0.15625
- wo_audio: bfloat16 [1536, 1536], P('seq'), may hold values from -0.875 to 0.875
Outputs:
- video_out: bfloat16 [65536, 1536], P(('grp', 'seq')), parts along dimension 0
- audio_out: bfloat16 [8192, 1536], P(('grp', 'seq')), parts along dimension 0
The draws below stay inside these ranges and needn't reach their ends.
There are 8 independent parts, one for each index of `grp`. The reference program is written for one: setup_inputs(seed, part) draws one part's arguments, and reference() takes and returns one part's arrays. A program takes and returns all parts, laid end to end along the dimension named above; an argument that names none is the same for every part. Nothing has to cross between parts.
All inputs are finite; a program needn't handle non-finite values.
Results may differ from the reference program's by a relative error of at most 0.035.
The reference program's roundings to bfloat16 on the way count: a program that leaves them out, or rounds other values in their place, can miss the bound.
Values may be sent and summed in bfloat16 or wider, within the bound.
A program may use at most 192 MiB of HBM per device.

```python
import jax
import jax.numpy as jnp
from jax import lax

D = 1536
HEADS = 12
HEAD_DIM = 128
INNER = 1536
SV_DEV = 512
SV = 8192
SA = 1024
N_SEQ = 16


def token_rows(key, count, width):
    first = jax.random.fold_in(key, 0)
    values = jax.random.normal(first, (count, width), jnp.float32)
    return jnp.clip(values, -6.0, 6.0)


def draw_video(key, part):
    key = jax.random.fold_in(key, 11)
    return token_rows(key, SV, D).astype(jnp.bfloat16)


def draw_audio(key, part):
    key = jax.random.fold_in(key, 23)
    return token_rows(key, SA, D).astype(jnp.bfloat16)


def levels(key, shape, cuts, low, largest):
    def one(dim, blocks):
        heights = jax.random.uniform(jax.random.fold_in(jax.random.fold_in(key, 6), dim), (blocks,), jnp.float32, low / len(cuts), largest / len(cuts))
        return jnp.repeat(jnp.exp(heights), shape[dim] // blocks).reshape((-1,) + (1,) * (len(shape) - dim - 1))

    level = one(*cuts[0])
    for cut in cuts[1:]:
        level = level * one(*cut)
    return level


def normal_values(key, shape, scale, reach, cuts=(), held_as=jnp.bfloat16):
    factor_of = levels(key, shape, cuts, -0.22, 0.18) if cuts else 1.0
    drawn = jax.random.normal(key, shape, jnp.float32) * scale * factor_of
    return jnp.minimum(jnp.maximum(drawn, -reach), reach).astype(held_as)


def setup_inputs(seed: int = 0, part: int = 0) -> dict:
    key_list = jax.random.split(jax.random.key(seed), 11)
    part_keys = jax.random.split(jax.random.fold_in(key_list[10], part), 11)
    video = draw_video(jax.random.fold_in(jax.random.fold_in(key_list[10], part), 71), part)
    audio = draw_audio(jax.random.fold_in(jax.random.fold_in(key_list[10], part), 71), part)
    wq_video = normal_values(key_list[2], (D, INNER), (2 * D ** -0.5), 0.3125)
    wk_video = normal_values(key_list[3], (D, INNER), D ** -0.5, 0.15625)
    wv_video = normal_values(key_list[4], (D, INNER), D ** -0.5, 0.15625)
    wo_video = normal_values(key_list[5], (INNER, D), (6 * INNER ** -0.5), 0.875)
    wq_audio = normal_values(key_list[6], (D, INNER), (2 * D ** -0.5), 0.3125, ((0, 16),))
    wk_audio = normal_values(key_list[7], (D, INNER), D ** -0.5, 0.15625, ((0, 16),))
    wv_audio = normal_values(key_list[8], (D, INNER), D ** -0.5, 0.15625, ((0, 16),))
    wo_audio = normal_values(key_list[9], (INNER, D), (6 * INNER ** -0.5), 0.875, ((0, 16),))
    return {"video": video, "audio": audio, "wq_video": wq_video, "wk_video": wk_video, "wv_video": wv_video, "wo_video": wo_video, "wq_audio": wq_audio, "wk_audio": wk_audio, "wv_audio": wv_audio, "wo_audio": wo_audio}


def by_heads(rows):
    return rows.reshape(rows.shape[0], HEADS, HEAD_DIM)


def project(rows, weight):
    return jnp.dot(rows, weight, preferred_element_type=jnp.float32).astype(jnp.bfloat16)


def reference(video, audio, wq_video, wk_video, wv_video, wo_video, wq_audio, wk_audio, wv_audio, wo_audio):
    temper = HEAD_DIM ** -0.5
    q_video = project(video, wq_video)
    k_video = project(video, wk_video)
    v_video = project(video, wv_video)
    q_audio = by_heads(project(audio, wq_audio)).astype(jnp.float32)
    k_audio = by_heads(project(audio, wk_audio)).astype(jnp.float32)
    v_audio = by_heads(project(audio, wv_audio)).astype(jnp.float32)

    def front_block(query_block):
        scores = jnp.einsum("qhd,khd->hqk", query_block.astype(jnp.float32), k_audio) * temper
        peak = jnp.max(scores, axis=-1, keepdims=True)
        expo_front = jnp.exp(scores - peak)
        sums = jnp.sum(expo_front, axis=-1)
        weights = expo_front.astype(jnp.bfloat16).astype(jnp.float32)
        blended = jnp.einsum("hqk,khd->qhd", weights, v_audio)
        attended = (blended / jnp.transpose(sums)[:, :, None]).astype(jnp.bfloat16)
        attended = attended.reshape(query_block.shape[0], HEADS * HEAD_DIM)
        return project(attended, wo_video)

    video_out = lax.map(front_block, q_video.reshape(N_SEQ, SV_DEV, HEADS, HEAD_DIM)).reshape(SV, D)

    def back_block(pair):
        key_block, value_block = pair
        scores = jnp.einsum("qhd,khd->hqk", q_audio, key_block.astype(jnp.float32)) * temper
        peak = jnp.max(scores, axis=-1)
        expo_back = jnp.exp(scores - peak[:, :, None])
        totals = jnp.sum(expo_back, axis=-1)
        weights = expo_back.astype(jnp.bfloat16).astype(jnp.float32)
        numerator = jnp.einsum("hqk,khd->qhd", weights, value_block.astype(jnp.float32))
        return numerator, peak, totals

    key_blocks = k_video.reshape(N_SEQ, SV_DEV, HEADS, HEAD_DIM)
    value_blocks = v_video.reshape(N_SEQ, SV_DEV, HEADS, HEAD_DIM)
    numerators, peaks, totals = lax.map(back_block, (key_blocks, value_blocks))
    global_peak = jnp.max(peaks, axis=0)
    factor = jnp.exp(peaks - global_peak[None])
    scaled_numer = (numerators * jnp.transpose(factor, (0, 2, 1))[:, :, :, None]).astype(jnp.bfloat16)
    scaled_total = (totals * factor).astype(jnp.bfloat16)
    numer_sum = jnp.sum(scaled_numer.astype(jnp.float32), axis=0)
    total_sum = jnp.sum(scaled_total.astype(jnp.float32), axis=0)
    attended = (numer_sum / jnp.transpose(total_sum)[:, :, None]).astype(jnp.bfloat16)
    audio_out = project(attended.reshape(SA, HEADS * HEAD_DIM), wo_audio)
    return video_out, audio_out
```

```python
import functools

import jax
import jax.numpy as jnp
from jax import lax
from jax.experimental import pallas as pl
from jax.experimental.pallas import tpu as pltpu
from jax.sharding import PartitionSpec as P

HEADS = 12
HEAD_DIM = 128
D = 1536
INNER = 1536
ROWS = 512
OWN = 64
PART = 384
STRIPE = 48
MESH = pl.DeviceIdType.MESH
F32 = jnp.float32
BF16 = jnp.bfloat16
ANY = pl.BlockSpec(memory_space=pl.ANY)


def place():
    s, g = lax.axis_index("seq"), lax.axis_index("grp")
    return s // 4, s % 4, g // 2, g % 2


def device(x, y, z, c):
    return (x * 4 + y, z * 2 + c)


def remote(src, dst, send, recv, to):
    return pltpu.make_async_remote_copy(
        src_ref=src, dst_ref=dst, send_sem=send, recv_sem=recv, device_id=to, device_id_type=MESH
    )


class Sems:
    def __init__(self, send, recv, local):
        self.send, self.recv, self.local = send, recv, local
        self.n_remote, self.n_local = 0, 0

    def remote(self, src, dst, to):
        i = self.n_remote
        self.n_remote += 1
        return remote(src, dst, self.send.at[i], self.recv.at[i], to)

    def copy(self, src, dst):
        i = self.n_local
        self.n_local += 1
        return pltpu.make_async_copy(src, dst, self.local.at[i])


def start(copies):
    for copy in copies:
        copy.start()
    return copies


def arrived(copies):
    for copy in copies:
        copy.wait_recv()


def left(copies):
    for copy in copies:
        copy.wait_send()


def greet(devices):
    barrier = pltpu.get_barrier_semaphore()
    for to in devices:
        pl.semaphore_signal(barrier, inc=1, device_id=to, device_id_type=MESH)
    pl.semaphore_wait(barrier, len(devices))


def gather_first(sems, buf, x, y, z, c):
    half = INNER // 2
    xr = x % 2
    pair = device(x + 1 - 2 * xr, y, z, c)
    ones = [sems.remote(buf.at[xr, y, c, :, :half], buf.at[xr, y, c, :, :half], pair)]
    twos = []
    for dy in (1, 3, 2):
        part = buf.at[xr, y, c, :, half:]
        twos.append(sems.remote(part, part, device(x, (y + dy) % 4, z, c)))
    return start(ones + twos)


def gather_second(sems, buf, x, y, z, c):
    half = INNER // 2
    xr = x % 2
    pair = device(x + 1 - 2 * xr, y, z, c)
    copies = []
    for dy in (1, 3, 2):
        part = buf.at[:, y, c, :, :half]
        copies.append(sems.remote(part, part, device(x, (y + dy) % 4, z, c)))
    part = buf.at[xr, :, c, :, half:]
    copies.append(sems.remote(part, part, pair))
    return start(copies)


def gather_third(sems, buf, x, y, z, c):
    part = buf.at[:, :, c]
    return start([sems.remote(part, part, device(x, y, z, 1 - c))])


def k1(
    video, audio, wq, wk, wv, aqw, akw, avw, aow,
    qo, ko, vo, gqo, owno, woo,
    wcol, arows, vid, wbuf, pres, gq, own, proj,
    send, recv, local,
):
    x, y, z, c = place()
    s = x * 4 + y
    xr = x % 2
    native = c == x // 2
    xd = jnp.where(native, x, 3 - x)
    cd = jnp.where(native, c, 1 - c)
    partner = device(3 - x, y, z, 1 - c)
    sibling = device(x, y, z, 1 - c)
    sems = Sems(send, recv, local)

    stripes = [
        sems.copy(
            w.at[pl.ds(pl.multiple_of(c * STRIPE, 16), STRIPE), pl.ds(pl.multiple_of(z * PART, 128), PART)],
            wcol.at[x, y, c, :, i * PART : (i + 1) * PART],
        )
        for i, w in enumerate((aqw, akw, avw, aow))
    ]
    own_audio = sems.copy(audio, arows.at[z])
    weights = [sems.copy(w, wbuf.at[i]) for i, w in enumerate((wq, wk, wv))]
    own_video = sems.copy(video, vid)
    start(stripes + [own_audio])

    xs = [device((x + d) % 4, y, z, c) for d in (1, 3, 2)]
    ys = [device(x, (y + d) % 4, z, c) for d in (1, 3, 2)]
    zs = [device(x, y, (z + d) % 4, c) for d in (1, 3, 2)]
    cross = [device(3 - x, y, (z + d) % 4, 1 - c) for d in range(4)]
    greet(xs + ys + zs + cross + [sibling])

    first, second, last = slice(0, 512), slice(512, 1152), slice(1152, 1536)
    for copy in stripes:
        copy.wait()
    mine = wcol.at[x, y, c]
    a_x = start([sems.remote(mine.at[:, first], mine.at[:, first], to) for to in xs])
    a_y = start([sems.remote(mine.at[:, second], mine.at[:, second], to) for to in ys])
    own_audio.wait()
    a_z = start([sems.remote(arows.at[z], arows.at[z], to) for to in zs])
    swap = sems.remote(video, vid, partner)
    pl.when(native)(own_video.start)
    pl.when(jnp.logical_not(native))(swap.start)
    start(weights)
    arrived(a_x)
    part = wcol.at[:, y, c, :, first]
    b_y = start([sems.remote(part, part, to) for to in ys])
    arrived(a_y)
    part = wcol.at[x, :, c, :, second]
    b_x = start([sems.remote(part, part, to) for to in xs])
    arrived(b_y)
    part = wcol.at[:, :, c, :, first]
    c_1 = start([sems.remote(part, part, sibling)])
    arrived(b_x)
    part = wcol.at[:, :, c, :, second]
    c_2 = start([sems.remote(part, part, sibling)])
    arrived(a_z)
    arrived(c_1)

    rows = arows[...].reshape(4 * OWN, D)
    to_owner = []
    slot_x = xd % 2
    for i in range(3):
        if i == 1:
            arrived(c_2)
        cols = slice(i * PART, (i + 1) * PART)
        weight = wcol[:, :, :, :, cols].reshape(D, PART)
        pres[i] = jnp.dot(rows, weight, preferred_element_type=F32).astype(BF16).reshape(4, OWN, PART)
        lanes = pl.ds(pl.multiple_of(z * PART, 128), PART)
        target = gq.at[slot_x, y, cd, :, lanes] if i == 0 else own.at[i - 1, :, lanes]
        group = []
        for dz in range(1, 4):
            zd = (z + dz) % 4
            group.append(sems.remote(pres.at[i, zd], target, device(xd, y, zd, cd)))
        start(group)
        here = sems.copy(pres.at[i, z], target)
        away = sems.remote(pres.at[i, z], target, device(xd, y, z, cd))
        pl.when(native)(here.start)
        pl.when(jnp.logical_not(native))(away.start)
        to_owner.append((group, here, away))

    def landed(i):
        group, here, away = to_owner[i]
        arrived(group)
        pl.when(native)(here.wait)
        pl.when(jnp.logical_not(native))(away.wait_recv)

    o_x = start([sems.remote(mine.at[:, last], mine.at[:, last], to) for to in xs])

    def project(i):
        weights[i].wait()

        @pl.loop(0, INNER // 256)
        def _(n):
            lanes = pl.ds(pl.multiple_of(n * 256, 256), 256)
            proj[i, :, lanes] = jnp.dot(vid[...], wbuf[i, :, lanes], preferred_element_type=F32).astype(BF16)

    landed(0)
    g_1 = gather_first(sems, gq, x, y, z, c)
    pl.when(native)(own_video.wait)
    pl.when(jnp.logical_not(native))(swap.wait_recv)
    project(0)
    outs = [sems.copy(proj.at[i], o) for i, o in enumerate((qo, ko, vo))]
    outs[0].start()
    arrived(g_1)
    g_2 = gather_second(sems, gq, x, y, z, c)
    arrived(o_x)
    part = wcol.at[:, y, c, :, last]
    o_y = start([sems.remote(part, part, to) for to in ys])
    project(1)
    outs[1].start()
    arrived(g_2)
    g_3 = gather_third(sems, gq, x, y, z, c)
    project(2)
    outs[2].start()
    landed(1)
    landed(2)
    own_out = sems.copy(own, owno)
    own_out.start()
    arrived(o_y)
    o_out = sems.copy(wcol.at[:, :, c, :, last], woo)
    o_out.start()
    arrived(g_3)
    q_out = sems.copy(gq, gqo)
    q_out.start()
    left(a_x + a_y + a_z + b_x + b_y + c_1 + c_2 + o_x + o_y + g_1 + g_2 + g_3)
    for group, here, away in to_owner:
        left(group)
        pl.when(jnp.logical_not(native))(away.wait_send)
    pl.when(jnp.logical_not(native))(swap.wait_send)
    for copy in outs + [own_out, o_out, q_out]:
        copy.wait()


def call_k1(*args):
    sds = jax.ShapeDtypeStruct
    return pl.pallas_call(
        k1,
        out_shape=[sds((ROWS, INNER), BF16)] * 3
        + [sds((2, 4, 2, OWN, INNER), BF16), sds((2, OWN, INNER), BF16), sds((4, 4, STRIPE, PART), BF16)],
        in_specs=[ANY] * 9,
        out_specs=[ANY] * 6,
        scratch_shapes=[
            pltpu.VMEM((4, 4, 2, STRIPE, 4 * PART), BF16),
            pltpu.VMEM((4, OWN, D), BF16),
            pltpu.VMEM((ROWS, D), BF16),
            pltpu.VMEM((3, D, INNER), BF16),
            pltpu.VMEM((3, 4, OWN, PART), BF16),
            pltpu.VMEM((2, 4, 2, OWN, INNER), BF16),
            pltpu.VMEM((2, OWN, INNER), BF16),
            pltpu.VMEM((3, ROWS, INNER), BF16),
            pltpu.SemaphoreType.DMA((64,)),
            pltpu.SemaphoreType.DMA((64,)),
            pltpu.SemaphoreType.DMA((32,)),
        ],
        compiler_params=pltpu.CompilerParams(collective_id=1, has_side_effects=True, vmem_limit_bytes=56 * 2**20),
        name="project_and_gather",
    )(*args)


SCALE = HEAD_DIM**-0.5 * 1.4426950408889634
HALF = INNER // 2


def lanes_of(h):
    return pl.ds(pl.multiple_of(h * HEAD_DIM, HEAD_DIM), HEAD_DIM)


def soft(q, k, v):
    s = lax.dot_general(q, k, (((1,), (1,)), ((), ())), preferred_element_type=F32)
    m = jnp.max(s, axis=-1, keepdims=True)
    p = jnp.exp2((s - m) * SCALE)
    t = jnp.sum(p, axis=-1, keepdims=True)
    n = jnp.dot(p.astype(BF16), v, preferred_element_type=F32)
    return (n / t).astype(BF16), m, t


def merge(dst, logs_dst, srcs, logs, first_head):
    ls = [l[...] for l in logs]
    peak = functools.reduce(jnp.maximum, ls)
    ws = [jnp.exp2(l - peak) for l in ls]
    total = functools.reduce(jnp.add, ws)
    if logs_dst is not None:
        logs_dst[...] = peak + jnp.log2(total)
    ws = [w / total for w in ws]
    for i in range(dst.shape[-1] // HEAD_DIM):
        cols = slice(i * HEAD_DIM, (i + 1) * HEAD_DIM)
        h = first_head + i
        parts = [w[:, h : h + 1] * s[:, cols].astype(F32) for w, s in zip(ws, srcs)]
        dst[:, cols] = functools.reduce(jnp.add, parts).astype(BF16)


def k2(
    qi, ki, vi, gqi, owni, wo, woc,
    video_out, audio_out,
    qkv, gq, gk, gv, wov, woa, nb, logs, ra, rla, rb1, rlb1, rb2, rlb2, lmb1, lmb2, rc1, rlc1, rc2, rlc2,
    aud, att, out, aout,
    send, recv, local,
):
    x, y, z, c = place()
    xr = x % 2
    native = c == x // 2
    partner = device(3 - x, y, z, 1 - c)
    sibling = device(x, y, z, 1 - c)
    pair = device(x + 1 - 2 * xr, y, z, c)
    ys = [device(x, (y + d) % 4, z, c) for d in (1, 3, 2)]
    zs = [device(x, y, (z + d) % 4, c) for d in (1, 3, 2)]
    sems = Sems(send, recv, local)

    own_k = sems.copy(owni.at[0], gk.at[xr, y, c])
    own_v = sems.copy(owni.at[1], gv.at[xr, y, c])
    q_in = sems.copy(gqi, gq)
    ins = [sems.copy(a, qkv.at[i]) for i, a in enumerate((qi, ki, vi))]
    wo_in = sems.copy(wo, wov)
    woc_in = sems.copy(woc, woa.at[z, :, :, c])
    start([own_k, own_v, q_in, ins[1], ins[2], woc_in, ins[0], wo_in])
    greet(ys + zs + [pair, sibling, partner])

    own_k.wait()
    k_1 = gather_first(sems, gk, x, y, z, c)
    own_v.wait()
    v_1 = gather_first(sems, gv, x, y, z, c)
    woc_in.wait()
    part = woa.at[z, :, :, c]
    o_z = start([sems.remote(part, part, to) for to in zs])
    logs[...] = jnp.zeros_like(logs)
    q_in.wait()
    ins[1].wait()
    ins[2].wait()

    def back(first, last):
        @pl.loop(first, last)
        def _(h):
            cols = lanes_of(h)
            k, v = qkv[1, :, cols], qkv[2, :, cols]
            for i in range(2):
                q = gq[i, :, :, :, cols].reshape(512, HEAD_DIM)
                n, m, t = soft(q, k, v)
                nb[i, :, :, :, cols] = n.reshape(4, 2, OWN, HEAD_DIM)
                l = (m * SCALE + jnp.log2(t)).reshape(4, 2, OWN, 1)
                lane = lax.broadcasted_iota(jnp.int32, (4, 2, OWN, 128), 3)
                logs[i] = jnp.where(lane == h, l, logs[i])

    back(0, 3)
    arrived(k_1)
    k_2 = gather_second(sems, gk, x, y, z, c)
    back(3, 6)
    arrived(v_1)
    v_2 = gather_second(sems, gv, x, y, z, c)
    back(6, 9)
    arrived(k_2)
    k_3 = gather_third(sems, gk, x, y, z, c)
    back(9, 12)
    arrived(v_2)
    v_3 = gather_third(sems, gv, x, y, z, c)

    r_a = start(
        [sems.remote(nb.at[:, :, 1 - c], ra, sibling), sems.remote(logs.at[:, :, 1 - c], rla, sibling)]
    )
    ins[0].wait()
    arrived(k_3)
    arrived(v_3)
    backs = []

    def front(first, last):
        @pl.loop(first, last)
        def _(h):
            cols = lanes_of(h)
            k = gk[:, :, :, :, cols].reshape(1024, HEAD_DIM)
            v = gv[:, :, :, :, cols].reshape(1024, HEAD_DIM)
            for i in range(2):
                rows = slice(i * 256, (i + 1) * 256)
                n, _, _ = soft(qkv[0, rows, cols], k, v)
                att[0, rows, cols] = n

        cols = slice(first * HEAD_DIM, last * HEAD_DIM)
        copy = sems.remote(att.at[0, :, cols], att.at[1, :, cols], partner)
        pl.when(jnp.logical_not(native))(copy.start)
        backs.append(copy)

    front(0, 3)
    arrived(r_a)

    @pl.loop(0, 8)
    def _(b):
        i, j = b // 4, b % 4
        mine, mine_l = nb.at[i, j, c], logs.at[i, j, c]
        merge(mine, mine_l, [mine, ra.at[i, j]], [mine_l, rla.at[i, j]], 0)

    r_b1 = start(
        [
            sems.remote(nb.at[1 - xr, :, c, :, :HALF], rb1, pair),
            sems.remote(logs.at[1 - xr, :, c], rlb1, pair),
        ]
    )
    r_b2 = []
    for i, d in enumerate((1, 3, 2)):
        yd = (y + d) % 4
        r_b2.append(sems.remote(nb.at[:, yd, c, :, HALF:], rb2.at[i], ys[i]))
        r_b2.append(sems.remote(logs.at[:, yd, c], rlb2.at[i], ys[i]))
    start(r_b2)
    front(3, 6)
    arrived(r_b1)
    arrived(r_b2)

    @pl.loop(0, 4)
    def _(j):
        mine = nb.at[xr, j, c, :, :HALF]
        merge(mine, lmb1.at[j], [mine, rb1.at[j]], [logs.at[xr, j, c], rlb1.at[j]], 0)

    @pl.loop(0, 2)
    def _(i):
        mine = nb.at[i, y, c, :, HALF:]
        merge(
            mine,
            lmb2.at[i],
            [mine] + [rb2.at[d, i] for d in range(3)],
            [logs.at[i, y, c]] + [rlb2.at[d, i] for d in range(3)],
            6,
        )

    r_c = []
    for i, d in enumerate((1, 3, 2)):
        yd = (y + d) % 4
        r_c.append(sems.remote(nb.at[xr, yd, c, :, :HALF], rc1.at[i], ys[i]))
        r_c.append(sems.remote(lmb1.at[yd], rlc1.at[i], ys[i]))
    r_c.append(sems.remote(nb.at[1 - xr, y, c, :, HALF:], rc2, pair))
    r_c.append(sems.remote(lmb2.at[1 - xr], rlc2, pair))
    start(r_c)
    front(6, 9)
    arrived(r_c)
    mine = nb.at[xr, y, c, :, :HALF]
    merge(
        aud.at[0, :, :HALF],
        None,
        [mine] + [rc1.at[d] for d in range(3)],
        [lmb1.at[y]] + [rlc1.at[d] for d in range(3)],
        0,
    )
    mine = nb.at[xr, y, c, :, HALF:]
    merge(aud.at[0, :, HALF:], None, [mine, rc2], [lmb2.at[xr], rlc2], 6)
    r_d = sems.remote(aud.at[0], aud.at[1], partner)
    pl.when(jnp.logical_not(native))(r_d.start)
    arrived(o_z)
    part = woa.at[:, :, :, c]
    o_c = start([sems.remote(part, part, sibling)])
    front(9, 12)

    which = jnp.where(native, 0, 1)
    pl.when(jnp.logical_not(native))(r_d.wait_recv)
    arrived(o_c)
    rows = aud[which]
    for i in range(4):
        weight = woa[i].reshape(D, PART)
        aout[:, i * PART : (i + 1) * PART] = jnp.dot(rows, weight, preferred_element_type=F32).astype(BF16)
    a_out = sems.copy(aout, audio_out)
    a_out.start()
    wo_in.wait()
    for copy in backs:
        pl.when(jnp.logical_not(native))(copy.wait_recv)
    v_out = []

    for n in range(6):
        cols = slice(n * 256, (n + 1) * 256)
        out[:, cols] = jnp.dot(att[which], wov[:, cols], preferred_element_type=F32).astype(BF16)
        copy = sems.copy(out.at[:, cols], video_out.at[:, cols])
        copy.start()
        v_out.append(copy)

    left(k_1 + k_2 + k_3 + v_1 + v_2 + v_3 + o_z + o_c + r_a + r_b1 + r_b2 + r_c)
    for copy in backs + [r_d]:
        pl.when(jnp.logical_not(native))(copy.wait_send)
    a_out.wait()
    for copy in v_out:
        copy.wait()


def call_k2(*args):
    sds = jax.ShapeDtypeStruct
    block = (2, 4, 2, OWN, INNER)
    return pl.pallas_call(
        k2,
        out_shape=[sds((ROWS, D), BF16), sds((OWN, D), BF16)],
        in_specs=[ANY] * 7,
        out_specs=[ANY] * 2,
        scratch_shapes=[
            pltpu.VMEM((3, ROWS, INNER), BF16),
            pltpu.VMEM(block, BF16),
            pltpu.VMEM(block, BF16),
            pltpu.VMEM(block, BF16),
            pltpu.VMEM((INNER, D), BF16),
            pltpu.VMEM((4, 4, 4, 2, STRIPE, PART), BF16),
            pltpu.VMEM(block, BF16),
            pltpu.VMEM((2, 4, 2, OWN, 128), F32),
            pltpu.VMEM((2, 4, OWN, INNER), BF16),
            pltpu.VMEM((2, 4, OWN, 128), F32),
            pltpu.VMEM((4, OWN, HALF), BF16),
            pltpu.VMEM((4, OWN, 128), F32),
            pltpu.VMEM((3, 2, OWN, HALF), BF16),
            pltpu.VMEM((3, 2, OWN, 128), F32),
            pltpu.VMEM((4, OWN, 128), F32),
            pltpu.VMEM((2, OWN, 128), F32),
            pltpu.VMEM((3, OWN, HALF), BF16),
            pltpu.VMEM((3, OWN, 128), F32),
            pltpu.VMEM((OWN, HALF), BF16),
            pltpu.VMEM((OWN, 128), F32),
            pltpu.VMEM((2, OWN, INNER), BF16),
            pltpu.VMEM((2, ROWS, INNER), BF16),
            pltpu.VMEM((ROWS, D), BF16),
            pltpu.VMEM((OWN, D), BF16),
            pltpu.SemaphoreType.DMA((64,)),
            pltpu.SemaphoreType.DMA((64,)),
            pltpu.SemaphoreType.DMA((32,)),
        ],
        compiler_params=pltpu.CompilerParams(collective_id=2, has_side_effects=True, vmem_limit_bytes=60 * 2**20),
        name="attend_and_merge",
    )(*args)


def on_device(
    video, audio, wq_video, wk_video, wv_video, wo_video, wq_audio, wk_audio, wv_audio, wo_audio
):
    q, k, v, gq, own, woc = call_k1(
        video, audio, wq_video, wk_video, wv_video, wq_audio, wk_audio, wv_audio, wo_audio
    )
    return tuple(call_k2(q, k, v, gq, own, wo_video, woc))


def solution(mesh):
    tokens, rows = P(("grp", "seq"), None), P("seq", None)
    in_specs = (tokens, tokens, P(), P(), P(), P(), rows, rows, rows, rows)
    return jax.shard_map(
        on_device, mesh=mesh, in_specs=in_specs, out_specs=(tokens, tokens), check_vma=False
    )
```

```python
import functools

import jax
import jax.numpy as jnp
from jax import lax
from jax.experimental import pallas as pl
from jax.experimental.pallas import tpu as pltpu
from jax.sharding import PartitionSpec as P

HEADS = 12
HEAD_DIM = 128
D = 1536
INNER = 1536
ROWS = 512
OWN = 64
PART = 384
STRIPE = 48
MESH = pl.DeviceIdType.MESH
F32 = jnp.float32
BF16 = jnp.bfloat16
ANY = pl.BlockSpec(memory_space=pl.ANY)


def place():
    s, g = lax.axis_index("seq"), lax.axis_index("grp")
    return s // 4, s % 4, g // 2, g % 2


def device(x, y, z, c):
    return (x * 4 + y, z * 2 + c)


def remote(src, dst, send, recv, to):
    return pltpu.make_async_remote_copy(
        src_ref=src, dst_ref=dst, send_sem=send, recv_sem=recv, device_id=to, device_id_type=MESH
    )


class Sems:
    def __init__(self, send, recv, local):
        self.send, self.recv, self.local = send, recv, local
        self.n_remote, self.n_local = 0, 0

    def remote(self, src, dst, to):
        i = self.n_remote
        self.n_remote += 1
        return remote(src, dst, self.send.at[i], self.recv.at[i], to)

    def copy(self, src, dst):
        i = self.n_local
        self.n_local += 1
        return pltpu.make_async_copy(src, dst, self.local.at[i])


def start(copies):
    for copy in copies:
        copy.start()
    return copies


def arrived(copies):
    for copy in copies:
        copy.wait_recv()


def left(copies):
    for copy in copies:
        copy.wait_send()


def greet(devices):
    barrier = pltpu.get_barrier_semaphore()
    for to in devices:
        pl.semaphore_signal(barrier, inc=1, device_id=to, device_id_type=MESH)
    pl.semaphore_wait(barrier, len(devices))


def gather_first(sems, buf, x, y, z, c):
    half = INNER // 2
    xr = x % 2
    pair = device(x + 1 - 2 * xr, y, z, c)
    ones = [sems.remote(buf.at[xr, y, c, :, :half], buf.at[xr, y, c, :, :half], pair)]
    twos = []
    for dy in (1, 3, 2):
        part = buf.at[xr, y, c, :, half:]
        twos.append(sems.remote(part, part, device(x, (y + dy) % 4, z, c)))
    return ones + twos


def gather_second(sems, buf, x, y, z, c):
    half = INNER // 2
    xr = x % 2
    pair = device(x + 1 - 2 * xr, y, z, c)
    copies = []
    for dy in (1, 3, 2):
        part = buf.at[:, y, c, :, :half]
        copies.append(sems.remote(part, part, device(x, (y + dy) % 4, z, c)))
    part = buf.at[xr, :, c, :, half:]
    copies.append(sems.remote(part, part, pair))
    return copies


def gather_third(sems, buf, x, y, z, c):
    part = buf.at[:, :, c]
    return [sems.remote(part, part, device(x, y, z, 1 - c))]


SCALE = HEAD_DIM**-0.5 * 1.4426950408889634
HALF = INNER // 2


def lanes_of(h):
    return pl.ds(pl.multiple_of(h * HEAD_DIM, HEAD_DIM), HEAD_DIM)


def soft(q, k, v):
    s = lax.dot_general(q, k, (((1,), (1,)), ((), ())), preferred_element_type=F32)
    m = jnp.max(s, axis=-1, keepdims=True)
    p = jnp.exp2((s - m) * SCALE)
    t = jnp.sum(p, axis=-1, keepdims=True)
    n = jnp.dot(p.astype(BF16), v, preferred_element_type=F32)
    return (n / t).astype(BF16), m, t


def merge(dst, logs_dst, srcs, logs, first_head):
    ls = [l[...] for l in logs]
    peak = functools.reduce(jnp.maximum, ls)
    ws = [jnp.exp2(l - peak) for l in ls]
    total = functools.reduce(jnp.add, ws)
    if logs_dst is not None:
        logs_dst[...] = peak + jnp.log2(total)
    ws = [w / total for w in ws]
    for i in range(dst.shape[-1] // HEAD_DIM):
        cols = slice(i * HEAD_DIM, (i + 1) * HEAD_DIM)
        h = first_head + i
        parts = [w[:, h : h + 1] * s[:, cols].astype(F32) for w, s in zip(ws, srcs)]
        dst[:, cols] = functools.reduce(jnp.add, parts).astype(BF16)


def attend(
    video, audio, wq, wk, wv, wo, aqw, akw, avw, aow,
    video_out, audio_out,
    wcol, arows, vid, wbuf, pres, gq, gk, gv, qkv, woa, nb, logs, ra, rla, rb1, rlb1, rb2, rlb2,
    lmb1, lmb2, rc1, rlc1, rc2, rlc2, aud, att, out, aout,
    send, recv, local,
):
    x, y, z, c = place()
    xr = x % 2
    native = c == x // 2
    guest = jnp.logical_not(native)
    xd = jnp.where(native, x, 3 - x)
    cd = jnp.where(native, c, 1 - c)
    partner = device(3 - x, y, z, 1 - c)
    sibling = device(x, y, z, 1 - c)
    pair = device(x + 1 - 2 * xr, y, z, c)
    xs = [device((x + d) % 4, y, z, c) for d in (1, 3, 2)]
    ys = [device(x, (y + d) % 4, z, c) for d in (1, 3, 2)]
    zs = [device(x, y, (z + d) % 4, c) for d in (1, 3, 2)]
    cross = [device(3 - x, y, (z + d) % 4, 1 - c) for d in range(4)]
    sems = Sems(send, recv, local)
    sent = []

    def push(copies):
        sent.extend(copies)
        return start(copies)

    stripes = [
        sems.copy(
            w.at[pl.ds(pl.multiple_of(c * STRIPE, 16), STRIPE), pl.ds(pl.multiple_of(z * PART, 128), PART)],
            wcol.at[x, y, c, :, i * PART : (i + 1) * PART],
        )
        for i, w in enumerate((aqw, akw, avw, aow))
    ]
    own_audio = sems.copy(audio, arows.at[z])
    weights = [sems.copy(w, wbuf.at[i]) for i, w in enumerate((wq, wk, wv))]
    halves = [slice(0, ROWS // 2), slice(ROWS // 2, ROWS)]
    own_video = [sems.copy(video.at[r], vid.at[r]) for r in halves]
    start(stripes + [own_audio])
    greet(xs + ys + zs + cross + [sibling])

    mine = wcol.at[x, y, c]

    def spread_first(cols, along):
        return push([sems.remote(mine.at[:, cols], mine.at[:, cols], to) for to in along])

    def spread_x_then(cols):
        part = wcol.at[:, y, c, :, cols]
        return push([sems.remote(part, part, to) for to in ys])

    def spread_y_then(cols):
        part = wcol.at[x, :, c, :, cols]
        return push([sems.remote(part, part, to) for to in xs])

    def spread_third(cols):
        part = wcol.at[:, :, c, :, cols]
        return push([sems.remote(part, part, sibling)])

    q_a, q_b, k_a, v_a, o_a = slice(0, 256), slice(256, 384), slice(384, 768), slice(768, 1152), slice(1152, 1536)
    for copy in stripes:
        copy.wait()
    sqa = spread_first(q_a, xs)
    sqb = spread_first(q_b, ys)
    own_audio.wait()
    a_z = push([sems.remote(arows.at[z], arows.at[z], to) for to in zs])
    sk = spread_first(k_a, xs)
    sv = spread_first(v_a, ys)
    start([weights[1], weights[2], weights[0]])

    @pl.when(native)
    def _():
        start(own_video)

    arrived(sqa)
    sqa = spread_x_then(q_a)
    arrived(sqb)
    sqb = spread_y_then(q_b)
    arrived(sk)
    sk = spread_x_then(k_a)
    arrived(sv)
    sv = spread_y_then(v_a)
    logs[...] = jnp.zeros_like(logs)
    arrived(sqa + sqb)
    sq = spread_third(slice(0, 384))
    swap = [sems.remote(video.at[r], vid.at[r], partner) for r in halves]

    @pl.when(guest)
    def _():
        start(swap)

    arrived(a_z)

    slot_x = xd % 2
    to_owner = []

    def project_audio(i, buf):
        rows = arows[...].reshape(4 * OWN, D)
        weight = wcol[:, :, :, :, i * PART : (i + 1) * PART].reshape(D, PART)
        pres[i] = jnp.dot(rows, weight, preferred_element_type=F32).astype(BF16).reshape(4, OWN, PART)
        target = buf.at[slot_x, y, cd, :, pl.ds(pl.multiple_of(z * PART, 128), PART)]
        group = push(
            [sems.remote(pres.at[i, (z + d) % 4], target, device(xd, y, (z + d) % 4, cd)) for d in (1, 2, 3)]
        )
        here = sems.copy(pres.at[i, z], target)
        away = sems.remote(pres.at[i, z], target, device(xd, y, z, cd))
        pl.when(native)(here.start)
        pl.when(guest)(away.start)
        to_owner.append((group, here, away))

    def landed(i):
        group, here, away = to_owner[i]
        arrived(group)
        pl.when(native)(here.wait)
        pl.when(guest)(away.wait_recv)

    arrived(sq)
    project_audio(0, gq)
    arrived(sk)
    sk = spread_third(k_a)
    arrived(sv)
    sv = spread_third(v_a)
    landed(0)
    q_1 = push(gather_first(sems, gq, x, y, z, c))
    arrived(sk)
    project_audio(1, gk)
    arrived(sv)
    project_audio(2, gv)

    def project(i, r):
        @pl.loop(0, INNER // 256)
        def _(n):
            lanes = pl.ds(pl.multiple_of(n * 256, 256), 256)
            qkv[i, halves[r], lanes] = jnp.dot(
                vid[halves[r], :], wbuf[i, :, lanes], preferred_element_type=F32
            ).astype(BF16)

    def video_half(r):
        pl.when(native)(own_video[r].wait)
        pl.when(guest)(swap[r].wait_recv)

    weights[1].wait()
    video_half(0)
    project(1, 0)
    arrived(q_1)
    q_2 = push(gather_second(sems, gq, x, y, z, c))
    landed(1)
    k_1 = push(gather_first(sems, gk, x, y, z, c))
    weights[2].wait()
    project(2, 0)
    landed(2)
    v_1 = push(gather_first(sems, gv, x, y, z, c))
    weights[0].wait()
    project(0, 0)
    so = spread_first(o_a, xs)
    arrived(q_2)
    q_3 = push(gather_third(sems, gq, x, y, z, c))
    arrived(k_1)
    k_2 = push(gather_second(sems, gk, x, y, z, c))
    video_half(1)
    project(0, 1)
    wo_in = sems.copy(wo, wbuf.at[0])
    wo_in.start()
    project(1, 1)
    arrived(v_1)
    v_2 = push(gather_second(sems, gv, x, y, z, c))
    arrived(so)
    so = spread_x_then(o_a)
    project(2, 1)
    arrived(q_3)

    def back(first, last):
        @pl.loop(first, last)
        def _(h):
            cols = lanes_of(h)
            k, v = qkv[1, :, cols], qkv[2, :, cols]
            half = first // 6
            for i in range(2):
                q = gq[i, :, :, :, cols].reshape(512, HEAD_DIM)
                n, m, t = soft(q, k, v)
                nb[i, :, :, :, cols] = n.reshape(4, 2, OWN, HEAD_DIM)
                l = (m * SCALE + jnp.log2(t)).reshape(4, 2, OWN, 1)
                lane = lax.broadcasted_iota(jnp.int32, (4, 2, OWN, 128), 3)
                logs[half, i] = jnp.where(lane == h, l, logs[half, i])

    def to_sibling(half):
        cols = slice(half * HALF, (half + 1) * HALF)
        return push(
            [
                sems.remote(nb.at[:, :, 1 - c, :, cols], ra.at[:, :, :, cols], sibling),
                sems.remote(logs.at[half, :, :, 1 - c], rla.at[half], sibling),
            ]
        )

    def merge_sibling(half):
        cols = slice(half * HALF, (half + 1) * HALF)

        @pl.loop(0, 8)
        def _(b):
            i, j = b // 4, b % 4
            part, part_l = nb.at[i, j, c, :, cols], logs.at[half, i, j, c]
            merge(part, part_l, [part, ra.at[i, j, :, cols]], [part_l, rla.at[half, i, j]], half * 6)

    def front(first, last):
        @pl.loop(first, last)
        def _(h):
            cols = lanes_of(h)
            k = gk[:, :, :, :, cols].reshape(1024, HEAD_DIM)
            v = gv[:, :, :, :, cols].reshape(1024, HEAD_DIM)
            for i in range(2):
                n, _, _ = soft(qkv[0, halves[i], cols], k, v)
                att[0, halves[i], cols] = n

        cols = slice(first * HEAD_DIM, last * HEAD_DIM)
        copy = sems.remote(att.at[0, :, cols], att.at[1, :, cols], partner)
        pl.when(guest)(copy.start)
        return copy

    back(0, 3)
    arrived(k_2)
    k_3 = push(gather_third(sems, gk, x, y, z, c))
    back(3, 6)
    r_a1 = to_sibling(0)
    arrived(so)
    o_part = woa.at[z, :, :, c]
    o_own = sems.copy(wcol.at[:, :, c, :, o_a], o_part)
    o_own.start()
    arrived(v_2)
    v_3 = push(gather_third(sems, gv, x, y, z, c))
    o_own.wait()
    o_z = push([sems.remote(o_part, o_part, to) for to in zs])
    back(6, 9)
    arrived(r_a1)
    merge_sibling(0)
    r_b1 = push(
        [
            sems.remote(nb.at[1 - xr, :, c, :, :HALF], rb1, pair),
            sems.remote(logs.at[0, 1 - xr, :, c], rlb1, pair),
        ]
    )
    back(9, 12)
    r_a2 = to_sibling(1)
    arrived(k_3)
    arrived(v_3)
    backs = [front(0, 3)]
    arrived(r_a2)
    merge_sibling(1)
    r_b2 = []
    for i, d in enumerate((1, 3, 2)):
        yd = (y + d) % 4
        r_b2.append(sems.remote(nb.at[:, yd, c, :, HALF:], rb2.at[i], ys[i]))
        r_b2.append(sems.remote(logs.at[1, :, yd, c], rlb2.at[i], ys[i]))
    push(r_b2)
    arrived(r_b1)

    @pl.loop(0, 4)
    def _(j):
        part = nb.at[xr, j, c, :, :HALF]
        merge(part, lmb1.at[j], [part, rb1.at[j]], [logs.at[0, xr, j, c], rlb1.at[j]], 0)

    r_c1 = []
    for i, d in enumerate((1, 3, 2)):
        yd = (y + d) % 4
        r_c1.append(sems.remote(nb.at[xr, yd, c, :, :HALF], rc1.at[i], ys[i]))
        r_c1.append(sems.remote(lmb1.at[yd], rlc1.at[i], ys[i]))
    push(r_c1)
    backs.append(front(3, 6))
    arrived(r_b2)

    @pl.loop(0, 2)
    def _(i):
        part = nb.at[i, y, c, :, HALF:]
        merge(
            part,
            lmb2.at[i],
            [part] + [rb2.at[d, i] for d in range(3)],
            [logs.at[1, i, y, c]] + [rlb2.at[d, i] for d in range(3)],
            6,
        )

    r_c2 = push(
        [
            sems.remote(nb.at[1 - xr, y, c, :, HALF:], rc2, pair),
            sems.remote(lmb2.at[1 - xr], rlc2, pair),
        ]
    )
    backs.append(front(6, 9))
    arrived(r_c1)
    merge(
        aud.at[0, :, :HALF],
        None,
        [nb.at[xr, y, c, :, :HALF]] + [rc1.at[d] for d in range(3)],
        [lmb1.at[y]] + [rlc1.at[d] for d in range(3)],
        0,
    )
    arrived(r_c2)
    merge(aud.at[0, :, HALF:], None, [nb.at[xr, y, c, :, HALF:], rc2], [lmb2.at[xr], rlc2], 6)
    r_d = sems.remote(aud.at[0], aud.at[1], partner)
    pl.when(guest)(r_d.start)
    arrived(o_z)
    part = woa.at[:, :, :, c]
    o_c = push([sems.remote(part, part, sibling)])
    backs.append(front(9, 12))

    which = jnp.where(native, 0, 1)
    pl.when(guest)(r_d.wait_recv)
    arrived(o_c)
    rows = aud[which]
    for i in range(4):
        weight = woa[i].reshape(D, PART)
        aout[:, i * PART : (i + 1) * PART] = jnp.dot(rows, weight, preferred_element_type=F32).astype(BF16)
    a_out = sems.copy(aout, audio_out)
    a_out.start()
    wo_in.wait()
    for copy in backs:
        pl.when(guest)(copy.wait_recv)
    v_out = []
    for n in range(6):
        cols = slice(n * 256, (n + 1) * 256)
        out[:, cols] = jnp.dot(att[which], wbuf[0, :, cols], preferred_element_type=F32).astype(BF16)
        copy = sems.copy(out.at[:, cols], video_out.at[:, cols])
        copy.start()
        v_out.append(copy)

    left(sent)

    @pl.when(guest)
    def _():
        left(swap + backs + [r_d] + [away for _, _, away in to_owner])

    a_out.wait()
    for copy in v_out:
        copy.wait()


def on_device(*args):
    sds = jax.ShapeDtypeStruct
    block = (2, 4, 2, OWN, INNER)
    return tuple(
        pl.pallas_call(
            attend,
            out_shape=[sds((ROWS, D), BF16), sds((OWN, D), BF16)],
            in_specs=[ANY] * 10,
            out_specs=[ANY] * 2,
            scratch_shapes=[
                pltpu.VMEM((4, 4, 2, STRIPE, 4 * PART), BF16),
                pltpu.VMEM((4, OWN, D), BF16),
                pltpu.VMEM((ROWS, D), BF16),
                pltpu.VMEM((3, D, INNER), BF16),
                pltpu.VMEM((3, 4, OWN, PART), BF16),
                pltpu.VMEM(block, BF16),
                pltpu.VMEM(block, BF16),
                pltpu.VMEM(block, BF16),
                pltpu.VMEM((3, ROWS, INNER), BF16),
                pltpu.VMEM((4, 4, 4, 2, STRIPE, PART), BF16),
                pltpu.VMEM(block, BF16),
                pltpu.VMEM((2, 2, 4, 2, OWN, 128), F32),
                pltpu.VMEM((2, 4, OWN, INNER), BF16),
                pltpu.VMEM((2, 2, 4, OWN, 128), F32),
                pltpu.VMEM((4, OWN, HALF), BF16),
                pltpu.VMEM((4, OWN, 128), F32),
                pltpu.VMEM((3, 2, OWN, HALF), BF16),
                pltpu.VMEM((3, 2, OWN, 128), F32),
                pltpu.VMEM((4, OWN, 128), F32),
                pltpu.VMEM((2, OWN, 128), F32),
                pltpu.VMEM((3, OWN, HALF), BF16),
                pltpu.VMEM((3, OWN, 128), F32),
                pltpu.VMEM((OWN, HALF), BF16),
                pltpu.VMEM((OWN, 128), F32),
                pltpu.VMEM((2, OWN, INNER), BF16),
                pltpu.VMEM((2, ROWS, INNER), BF16),
                pltpu.VMEM((ROWS, D), BF16),
                pltpu.VMEM((OWN, D), BF16),
                pltpu.SemaphoreType.DMA((128,)),
                pltpu.SemaphoreType.DMA((128,)),
                pltpu.SemaphoreType.DMA((32,)),
            ],
            compiler_params=pltpu.CompilerParams(
                collective_id=1, has_side_effects=True, vmem_limit_bytes=60 * 2**20
            ),
            name="attend",
        )(*args)
    )


def solution(mesh):
    tokens, rows = P(("grp", "seq"), None), P("seq", None)
    in_specs = (tokens, tokens, P(), P(), P(), P(), rows, rows, rows, rows)
    return jax.shard_map(
        on_device, mesh=mesh, in_specs=in_specs, out_specs=(tokens, tokens), check_vma=False
    )
```

```python
import functools

import jax
import jax.numpy as jnp
from jax import lax
from jax.experimental import pallas as pl
from jax.experimental.pallas import tpu as pltpu
from jax.sharding import PartitionSpec as P

HEADS = 12
HEAD_DIM = 128
D = 1536
INNER = 1536
ROWS = 512
OWN = 64
PART = 384
STRIPE = 48
MESH = pl.DeviceIdType.MESH
F32 = jnp.float32
BF16 = jnp.bfloat16
ANY = pl.BlockSpec(memory_space=pl.ANY)


def place():
    s, g = lax.axis_index("seq"), lax.axis_index("grp")
    return s // 4, s % 4, g // 2, g % 2


def device(x, y, z, c):
    return (x * 4 + y, z * 2 + c)


def remote(src, dst, send, recv, to):
    return pltpu.make_async_remote_copy(
        src_ref=src, dst_ref=dst, send_sem=send, recv_sem=recv, device_id=to, device_id_type=MESH
    )


class Sems:
    def __init__(self, send, recv, local):
        self.send, self.recv, self.local = send, recv, local
        self.n_remote, self.n_local = 0, 0

    def remote(self, src, dst, to):
        i = self.n_remote
        self.n_remote += 1
        return remote(src, dst, self.send.at[i], self.recv.at[i], to)

    def copy(self, src, dst):
        i = self.n_local
        self.n_local += 1
        return pltpu.make_async_copy(src, dst, self.local.at[i])


def start(copies):
    for copy in copies:
        copy.start()
    return copies


def arrived(copies):
    for copy in copies:
        copy.wait_recv()


def left(copies):
    for copy in copies:
        copy.wait_send()


def greet(devices):
    barrier = pltpu.get_barrier_semaphore()
    for to in devices:
        pl.semaphore_signal(barrier, inc=1, device_id=to, device_id_type=MESH)
    pl.semaphore_wait(barrier, len(devices))


def gather_first(sems, buf, x, y, z, c):
    half = INNER // 2
    xr = x % 2
    pair = device(x + 1 - 2 * xr, y, z, c)
    ones = [sems.remote(buf.at[xr, y, c, :, :half], buf.at[xr, y, c, :, :half], pair)]
    twos = []
    for dy in (1, 3, 2):
        part = buf.at[xr, y, c, :, half:]
        twos.append(sems.remote(part, part, device(x, (y + dy) % 4, z, c)))
    return ones + twos


def gather_second(sems, buf, x, y, z, c):
    half = INNER // 2
    xr = x % 2
    pair = device(x + 1 - 2 * xr, y, z, c)
    copies = []
    for dy in (1, 3, 2):
        part = buf.at[:, y, c, :, :half]
        copies.append(sems.remote(part, part, device(x, (y + dy) % 4, z, c)))
    part = buf.at[xr, :, c, :, half:]
    copies.append(sems.remote(part, part, pair))
    return copies


def gather_third(sems, buf, x, y, z, c):
    part = buf.at[:, :, c]
    return [sems.remote(part, part, device(x, y, z, 1 - c))]


SCALE = HEAD_DIM**-0.5 * 1.4426950408889634
HALF = INNER // 2


def lanes_of(h):
    return pl.ds(pl.multiple_of(h * HEAD_DIM, HEAD_DIM), HEAD_DIM)


def soft(q, k, v):
    s = lax.dot_general(q, k, (((1,), (1,)), ((), ())), preferred_element_type=F32)
    m = jnp.max(s, axis=-1, keepdims=True)
    p = jnp.exp2((s - m) * SCALE)
    t = jnp.sum(p, axis=-1, keepdims=True)
    n = jnp.dot(p.astype(BF16), v, preferred_element_type=F32)
    return (n / t).astype(BF16), m, t


def merge(dst, logs_dst, srcs, logs, first_head):
    ls = [l[...] for l in logs]
    peak = functools.reduce(jnp.maximum, ls)
    ws = [jnp.exp2(l - peak) for l in ls]
    total = functools.reduce(jnp.add, ws)
    if logs_dst is not None:
        logs_dst[...] = peak + jnp.log2(total)
    ws = [w / total for w in ws]
    for i in range(dst.shape[-1] // HEAD_DIM):
        cols = slice(i * HEAD_DIM, (i + 1) * HEAD_DIM)
        h = first_head + i
        parts = [w[:, h : h + 1] * s[:, cols].astype(F32) for w, s in zip(ws, srcs)]
        dst[:, cols] = functools.reduce(jnp.add, parts).astype(BF16)


def attend(
    video, audio, wq, wk, wv, wo, aqw, akw, avw, aow,
    video_out, audio_out,
    wcol, arows, vid, wbuf, pres, gq, gk, gv, qkv, woa, nb, logs, ra, rla, rb1, rlb1, rb2, rlb2,
    lmb1, lmb2, rc1, rlc1, rc2, rlc2, aud, att, out, aout,
    send, recv, local,
):
    x, y, z, c = place()
    xr = x % 2
    native = c == x // 2
    guest = jnp.logical_not(native)
    xd = jnp.where(native, x, 3 - x)
    cd = jnp.where(native, c, 1 - c)
    partner = device(3 - x, y, z, 1 - c)
    sibling = device(x, y, z, 1 - c)
    pair = device(x + 1 - 2 * xr, y, z, c)
    xs = [device((x + d) % 4, y, z, c) for d in (1, 3, 2)]
    ys = [device(x, (y + d) % 4, z, c) for d in (1, 3, 2)]
    zs = [device(x, y, (z + d) % 4, c) for d in (1, 3, 2)]
    cross = [device(3 - x, y, (z + d) % 4, 1 - c) for d in range(4)]
    sems = Sems(send, recv, local)
    sent = []

    def push(copies):
        sent.extend(copies)
        return start(copies)

    stripes = [
        sems.copy(
            w.at[pl.ds(pl.multiple_of(c * STRIPE, 16), STRIPE), pl.ds(pl.multiple_of(z * PART, 128), PART)],
            wcol.at[x, y, c, :, i * PART : (i + 1) * PART],
        )
        for i, w in enumerate((aqw, akw, avw, aow))
    ]
    own_audio = sems.copy(audio, arows.at[z])
    weights = [sems.copy(w, wbuf.at[i]) for i, w in enumerate((wq, wk, wv))]
    halves = [slice(0, ROWS // 2), slice(ROWS // 2, ROWS)]
    own_video = [sems.copy(video.at[r], vid.at[r]) for r in halves]
    start(stripes + [own_audio])
    greet(xs + ys + zs + cross + [sibling])

    mine = wcol.at[x, y, c]

    def spread_first(cols, along):
        return push([sems.remote(mine.at[:, cols], mine.at[:, cols], to) for to in along])

    def spread_x_then(cols):
        part = wcol.at[:, y, c, :, cols]
        return push([sems.remote(part, part, to) for to in ys])

    def spread_y_then(cols):
        part = wcol.at[x, :, c, :, cols]
        return push([sems.remote(part, part, to) for to in xs])

    def spread_third(cols):
        part = wcol.at[:, :, c, :, cols]
        return push([sems.remote(part, part, sibling)])

    q_a, q_b, k_a, v_a, o_a = slice(0, 256), slice(256, 384), slice(384, 768), slice(768, 1152), slice(1152, 1536)
    for copy in stripes:
        copy.wait()
    sqa = spread_first(q_a, xs)
    sqb = spread_first(q_b, ys)
    own_audio.wait()
    a_z = push([sems.remote(arows.at[z], arows.at[z], to) for to in zs])
    sk = spread_first(k_a, xs)
    sv = spread_first(v_a, ys)
    start([weights[1], weights[2], weights[0]])

    @pl.when(native)
    def _():
        start(own_video)

    arrived(sqa)
    sqa = spread_x_then(q_a)
    arrived(sqb)
    sqb = spread_y_then(q_b)
    swap = [sems.remote(video.at[r], vid.at[r], partner) for r in halves]

    @pl.when(guest)
    def _():
        start(swap)

    arrived(sk)
    sk = spread_x_then(k_a)
    arrived(sv)
    sv = spread_y_then(v_a)
    logs[...] = jnp.zeros_like(logs)
    arrived(sqa + sqb)
    sq = spread_third(slice(0, 384))
    arrived(a_z)

    slot_x = xd % 2
    to_owner = []

    def project_audio(i, buf):
        rows = arows[...].reshape(4 * OWN, D)
        weight = wcol[:, :, :, :, i * PART : (i + 1) * PART].reshape(D, PART)
        pres[i] = jnp.dot(rows, weight, preferred_element_type=F32).astype(BF16).reshape(4, OWN, PART)
        target = buf.at[slot_x, y, cd, :, pl.ds(pl.multiple_of(z * PART, 128), PART)]
        group = push(
            [sems.remote(pres.at[i, (z + d) % 4], target, device(xd, y, (z + d) % 4, cd)) for d in (1, 2, 3)]
        )
        here = sems.copy(pres.at[i, z], target)
        away = sems.remote(pres.at[i, z], target, device(xd, y, z, cd))
        pl.when(native)(here.start)
        pl.when(guest)(away.start)
        to_owner.append((group, here, away))

    def landed(i):
        group, here, away = to_owner[i]
        arrived(group)
        pl.when(native)(here.wait)
        pl.when(guest)(away.wait_recv)

    arrived(sq)
    project_audio(0, gq)
    arrived(sk)
    sk = spread_third(k_a)
    arrived(sv)
    sv = spread_third(v_a)
    landed(0)
    q_1 = push(gather_first(sems, gq, x, y, z, c))
    arrived(sk)
    project_audio(1, gk)
    arrived(sv)
    project_audio(2, gv)

    def project(i, r):
        @pl.loop(0, INNER // 256)
        def _(n):
            lanes = pl.ds(pl.multiple_of(n * 256, 256), 256)
            qkv[i, halves[r], lanes] = jnp.dot(
                vid[halves[r], :], wbuf[i, :, lanes], preferred_element_type=F32
            ).astype(BF16)

    def video_half(r):
        pl.when(native)(own_video[r].wait)
        pl.when(guest)(swap[r].wait_recv)

    weights[1].wait()
    video_half(0)
    project(1, 0)
    arrived(q_1)
    q_2 = push(gather_second(sems, gq, x, y, z, c))
    landed(1)
    k_1 = push(gather_first(sems, gk, x, y, z, c))
    weights[2].wait()
    project(2, 0)
    landed(2)
    v_1 = push(gather_first(sems, gv, x, y, z, c))
    weights[0].wait()
    project(0, 0)
    so = spread_first(o_a, xs)
    arrived(q_2)
    q_3 = push(gather_third(sems, gq, x, y, z, c))
    arrived(k_1)
    k_2 = push(gather_second(sems, gk, x, y, z, c))
    video_half(1)
    project(0, 1)
    wo_in = sems.copy(wo, wbuf.at[0])
    wo_in.start()
    project(1, 1)
    arrived(v_1)
    v_2 = push(gather_second(sems, gv, x, y, z, c))
    arrived(so)
    so = spread_x_then(o_a)
    project(2, 1)
    arrived(q_3)

    def back(first, last):
        @pl.loop(first, last)
        def _(h):
            cols = lanes_of(h)
            k, v = qkv[1, :, cols], qkv[2, :, cols]
            half = first // 6
            for i in range(2):
                q = gq[i, :, :, :, cols].reshape(512, HEAD_DIM)
                n, m, t = soft(q, k, v)
                nb[i, :, :, :, cols] = n.reshape(4, 2, OWN, HEAD_DIM)
                l = (m * SCALE + jnp.log2(t)).reshape(4, 2, OWN, 1)
                lane = lax.broadcasted_iota(jnp.int32, (4, 2, OWN, 128), 3)
                logs[half, i] = jnp.where(lane == h, l, logs[half, i])

    def to_sibling(half):
        cols = slice(half * HALF, (half + 1) * HALF)
        return push(
            [
                sems.remote(nb.at[:, :, 1 - c, :, cols], ra.at[:, :, :, cols], sibling),
                sems.remote(logs.at[half, :, :, 1 - c], rla.at[half], sibling),
            ]
        )

    def merge_sibling(half):
        cols = slice(half * HALF, (half + 1) * HALF)

        @pl.loop(0, 8)
        def _(b):
            i, j = b // 4, b % 4
            part, part_l = nb.at[i, j, c, :, cols], logs.at[half, i, j, c]
            merge(part, part_l, [part, ra.at[i, j, :, cols]], [part_l, rla.at[half, i, j]], half * 6)

    def front(first, last):
        @pl.loop(first, last)
        def _(h):
            cols = lanes_of(h)
            k = gk[:, :, :, :, cols].reshape(1024, HEAD_DIM)
            v = gv[:, :, :, :, cols].reshape(1024, HEAD_DIM)
            for i in range(2):
                n, _, _ = soft(qkv[0, halves[i], cols], k, v)
                att[0, halves[i], cols] = n

        cols = slice(first * HEAD_DIM, last * HEAD_DIM)
        copy = sems.remote(att.at[0, :, cols], att.at[1, :, cols], partner)
        pl.when(guest)(copy.start)
        return copy

    back(0, 3)
    arrived(k_2)
    k_3 = push(gather_third(sems, gk, x, y, z, c))
    back(3, 6)
    r_a1 = to_sibling(0)
    arrived(so)
    o_part = woa.at[z, :, :, c]
    o_own = sems.copy(wcol.at[:, :, c, :, o_a], o_part)
    o_own.start()
    arrived(v_2)
    v_3 = push(gather_third(sems, gv, x, y, z, c))
    o_own.wait()
    o_z = push([sems.remote(o_part, o_part, to) for to in zs])
    back(6, 9)
    arrived(r_a1)
    merge_sibling(0)
    r_b1 = push(
        [
            sems.remote(nb.at[1 - xr, :, c, :, :HALF], rb1, pair),
            sems.remote(logs.at[0, 1 - xr, :, c], rlb1, pair),
        ]
    )
    back(9, 12)
    r_a2 = to_sibling(1)
    arrived(k_3)
    arrived(v_3)
    backs = [front(0, 3)]
    arrived(r_a2)
    merge_sibling(1)
    r_b2 = []
    for i, d in enumerate((1, 3, 2)):
        yd = (y + d) % 4
        r_b2.append(sems.remote(nb.at[:, yd, c, :, HALF:], rb2.at[i], ys[i]))
        r_b2.append(sems.remote(logs.at[1, :, yd, c], rlb2.at[i], ys[i]))
    push(r_b2)
    arrived(r_b1)

    @pl.loop(0, 4)
    def _(j):
        part = nb.at[xr, j, c, :, :HALF]
        merge(part, lmb1.at[j], [part, rb1.at[j]], [logs.at[0, xr, j, c], rlb1.at[j]], 0)

    r_c1 = []
    for i, d in enumerate((1, 3, 2)):
        yd = (y + d) % 4
        r_c1.append(sems.remote(nb.at[xr, yd, c, :, :HALF], rc1.at[i], ys[i]))
        r_c1.append(sems.remote(lmb1.at[yd], rlc1.at[i], ys[i]))
    push(r_c1)
    backs.append(front(3, 6))
    arrived(r_b2)

    @pl.loop(0, 2)
    def _(i):
        part = nb.at[i, y, c, :, HALF:]
        merge(
            part,
            lmb2.at[i],
            [part] + [rb2.at[d, i] for d in range(3)],
            [logs.at[1, i, y, c]] + [rlb2.at[d, i] for d in range(3)],
            6,
        )

    r_c2 = push(
        [
            sems.remote(nb.at[1 - xr, y, c, :, HALF:], rc2, pair),
            sems.remote(lmb2.at[1 - xr], rlc2, pair),
        ]
    )
    backs.append(front(6, 9))
    arrived(r_c1)
    merge(
        aud.at[0, :, :HALF],
        None,
        [nb.at[xr, y, c, :, :HALF]] + [rc1.at[d] for d in range(3)],
        [lmb1.at[y]] + [rlc1.at[d] for d in range(3)],
        0,
    )
    arrived(r_c2)
    merge(aud.at[0, :, HALF:], None, [nb.at[xr, y, c, :, HALF:], rc2], [lmb2.at[xr], rlc2], 6)
    r_d = sems.remote(aud.at[0], aud.at[1], partner)
    pl.when(guest)(r_d.start)
    arrived(o_z)
    part = woa.at[:, :, :, c]
    o_c = push([sems.remote(part, part, sibling)])
    backs.append(front(9, 12))

    which = jnp.where(native, 0, 1)
    pl.when(guest)(r_d.wait_recv)
    arrived(o_c)
    rows = aud[which]
    for i in range(4):
        weight = woa[i].reshape(D, PART)
        aout[:, i * PART : (i + 1) * PART] = jnp.dot(rows, weight, preferred_element_type=F32).astype(BF16)
    a_out = sems.copy(aout, audio_out)
    a_out.start()
    wo_in.wait()
    for copy in backs:
        pl.when(guest)(copy.wait_recv)
    v_out = []
    for n in range(6):
        cols = slice(n * 256, (n + 1) * 256)
        out[:, cols] = jnp.dot(att[which], wbuf[0, :, cols], preferred_element_type=F32).astype(BF16)
        copy = sems.copy(out.at[:, cols], video_out.at[:, cols])
        copy.start()
        v_out.append(copy)

    left(sent)

    @pl.when(guest)
    def _():
        left(swap + backs + [r_d] + [away for _, _, away in to_owner])

    a_out.wait()
    for copy in v_out:
        copy.wait()


def on_device(*args):
    sds = jax.ShapeDtypeStruct
    block = (2, 4, 2, OWN, INNER)
    return tuple(
        pl.pallas_call(
            attend,
            out_shape=[sds((ROWS, D), BF16), sds((OWN, D), BF16)],
            in_specs=[ANY] * 10,
            out_specs=[ANY] * 2,
            scratch_shapes=[
                pltpu.VMEM((4, 4, 2, STRIPE, 4 * PART), BF16),
                pltpu.VMEM((4, OWN, D), BF16),
                pltpu.VMEM((ROWS, D), BF16),
                pltpu.VMEM((3, D, INNER), BF16),
                pltpu.VMEM((3, 4, OWN, PART), BF16),
                pltpu.VMEM(block, BF16),
                pltpu.VMEM(block, BF16),
                pltpu.VMEM(block, BF16),
                pltpu.VMEM((3, ROWS, INNER), BF16),
                pltpu.VMEM((4, 4, 4, 2, STRIPE, PART), BF16),
                pltpu.VMEM(block, BF16),
                pltpu.VMEM((2, 2, 4, 2, OWN, 128), F32),
                pltpu.VMEM((2, 4, OWN, INNER), BF16),
                pltpu.VMEM((2, 2, 4, OWN, 128), F32),
                pltpu.VMEM((4, OWN, HALF), BF16),
                pltpu.VMEM((4, OWN, 128), F32),
                pltpu.VMEM((3, 2, OWN, HALF), BF16),
                pltpu.VMEM((3, 2, OWN, 128), F32),
                pltpu.VMEM((4, OWN, 128), F32),
                pltpu.VMEM((2, OWN, 128), F32),
                pltpu.VMEM((3, OWN, HALF), BF16),
                pltpu.VMEM((3, OWN, 128), F32),
                pltpu.VMEM((OWN, HALF), BF16),
                pltpu.VMEM((OWN, 128), F32),
                pltpu.VMEM((2, OWN, INNER), BF16),
                pltpu.VMEM((2, ROWS, INNER), BF16),
                pltpu.VMEM((ROWS, D), BF16),
                pltpu.VMEM((OWN, D), BF16),
                pltpu.SemaphoreType.DMA((128,)),
                pltpu.SemaphoreType.DMA((128,)),
                pltpu.SemaphoreType.DMA((32,)),
            ],
            compiler_params=pltpu.CompilerParams(
                collective_id=1, has_side_effects=True, vmem_limit_bytes=60 * 2**20
            ),
            name="attend",
        )(*args)
    )


def solution(mesh):
    tokens, rows = P(("grp", "seq"), None), P("seq", None)
    in_specs = (tokens, tokens, P(), P(), P(), P(), rows, rows, rows, rows)
    return jax.shard_map(
        on_device, mesh=mesh, in_specs=in_specs, out_specs=(tokens, tokens), check_vma=False
    )
```
